32 devices in a mesh: pb: 8 (over z, x), ao: 4 (over y, core).
Axes of the slice: x: 2, y: 2, z: 4, core: 2. Of those that a mesh axis runs over, the one named last changes fastest.
Arguments:
- queries: bfloat16 [8192, 128], P('pb'), may hold values from -4 to 4
- centres: bfloat16 [8192, 128], P(('pb', 'ao')), may hold values from -4 to 4
- coefs: bfloat16 [8192, 4096], P('pb', 'ao'), may hold values from -3 to 3
- pattern: int32 [8, 5], replicated, may hold values from 0 to 1, as said below
Outputs:
- scores: bfloat16 [8192, 4096], P('pb', 'ao')
The draws below stay inside these ranges and needn't reach their ends.
Inputs may be any that keep to these rules, and one draw needn't show every extreme that they name: pattern[i, j] tells whether query block i lists centre block i + j - 2; it is 0 where that block lies outside 0 to 7, and 1 for j = 2.
All inputs are finite; a program needn't handle non-finite values.
Results may differ from the reference program's by a relative error of at most 0.0049.
Values may be sent and summed in bfloat16 or wider, within the bound.
No kernel may reach another device: no remote copies, remote signals or barrier semaphores. Data moves between devices by JAX's collectives and lax.ppermute only.
A program may use at most 64 MiB of HBM per device.

```python
import math
import jax
import jax.numpy as jnp
from jax import lax

F = 128
OUT = 4096
CBS = 1024
HALF = 2
QDEV = 1024
NQB = 8
BAND = 5
NQ = 8192
NC = 8192


def coordinates(key, count, salt):
    base = jax.random.fold_in(key, salt)
    values = jnp.clip(jax.random.normal(jax.random.fold_in(base, 1), (count, F), jnp.float32), -4.0, 4.0)
    spread = jnp.exp(jax.random.uniform(jax.random.fold_in(base, 2), (count, 1), jnp.float32, math.log(0.5), 0.0))
    return (values * spread).astype(jnp.bfloat16)


def draw_queries(key, part):
    return coordinates(key, NQ, 101)


def draw_centres(key, part):
    return coordinates(key, NC, 202)


def draw_pattern(key, part):
    level = jax.random.randint(jax.random.fold_in(key, 303), (NQB, 1), 1, 4)
    coin = jax.random.randint(jax.random.fold_in(key, 304), (NQB, BAND), 0, 3)
    listed = (coin < level).astype(jnp.int32)
    block_ids = jnp.arange(NQB, dtype=jnp.int32)[:, None]
    shifts = jnp.arange(BAND, dtype=jnp.int32)[None, :] - HALF
    target = block_ids + shifts
    inside = (target >= 0) & (target < NQB)
    result = jnp.where(shifts == 0, 1, jnp.where(inside, listed, 0))
    return result.astype(jnp.int32)


def block_scale(own_key, shape, pieces, low, high):
    factor_of, own = 1.0, jax.random.fold_in(own_key, 6)
    for dim, shards_of in pieces:
        draws = jnp.exp(jax.random.uniform(jax.random.fold_in(own, dim), (shards_of,), jnp.float32, low / len(pieces), high / len(pieces)))
        factor_of = factor_of * jnp.repeat(draws, shape[dim] // shards_of).reshape([-1 if axis == dim else 1 for axis in range(len(shape))])
    return factor_of


def gaussian(stream_key, shape, scale, limit, split=(), kind=jnp.bfloat16):
    level = block_scale(stream_key, shape, split, -0.22, 0.18) if split else 1.0
    values = jax.random.normal(stream_key, shape, jnp.float32) * scale * level
    return jnp.minimum(jnp.maximum(values, -limit), limit).astype(kind)


def setup_inputs(seed: int = 0) -> dict:
    splits = jax.random.split(jax.random.key(seed), 5)
    queries = draw_queries(jax.random.fold_in(splits[4], 71), 0)
    centres = draw_centres(jax.random.fold_in(splits[4], 71), 0)
    coefs = gaussian(splits[2], (NC, OUT), 0.5, 3.0, ((0, 8), (1, 4)))
    pattern = draw_pattern(jax.random.fold_in(splits[4], 71), 0)
    return dict(queries=queries, centres=centres, coefs=coefs, pattern=pattern)


RADIUS_FACTOR = 1.3

def wendland_block(query_rows, query_norm, centre_rows):
    centre_wide = centre_rows.astype(jnp.float32)
    centre_norm = lax.optimization_barrier(jnp.sum(centre_wide * centre_wide, axis=1))[None, :]
    cross = jnp.dot(query_rows, centre_rows.T, preferred_element_type=jnp.float32)
    dist = jnp.sqrt(query_norm + centre_norm - 2.0 * cross)
    scaled = dist / (RADIUS_FACTOR * math.sqrt(query_rows.shape[1]))
    inner = jnp.maximum(1.0 - scaled, 0.0)
    return inner * inner * inner * inner * (4.0 * scaled + 1.0)

def reference(queries, centres, coefs, pattern):

    def one_block(block_index):
        query_rows = lax.dynamic_slice_in_dim(queries, (block_index * QDEV).astype(jnp.int32), QDEV, 0)
        query_wide = query_rows.astype(jnp.float32)
        query_norm = lax.optimization_barrier(jnp.sum(query_wide * query_wide, axis=1))[:, None]

        def add_block(offset, accumulated):
            offset = jnp.asarray(offset).astype(jnp.int32)
            target = block_index + offset - HALF
            clamped = jnp.clip(target, 0, NQB - 1).astype(jnp.int32)
            centre_rows = lax.dynamic_slice_in_dim(centres, clamped * CBS, CBS, 0)
            coef_rows = lax.dynamic_slice_in_dim(coefs, clamped * CBS, CBS, 0)
            listed = pattern[block_index, offset]

            def compute(current):
                kern = (wendland_block(query_rows, query_norm, centre_rows) * listed.astype(jnp.float32)).astype(jnp.bfloat16)
                return current + jnp.dot(kern, coef_rows, preferred_element_type=jnp.float32)
            return lax.cond(listed > 0, compute, lambda current: current, accumulated)
        accumulated = lax.fori_loop(0, BAND, add_block, jnp.zeros((QDEV, OUT), jnp.float32))
        return accumulated.astype(jnp.bfloat16)
    blocks = lax.map(one_block, jnp.arange(NQB, dtype=jnp.int32))
    return blocks.reshape(NQ, OUT)
```

```python
import functools
import math

import jax
import jax.numpy as jnp
from jax import lax
from jax.experimental import pallas as pl
from jax.experimental.pallas import tpu as pltpu
from jax.sharding import PartitionSpec as P

RADIUS_FACTOR = 1.3
VMEM_LIMIT = 24 * 1024 * 1024
BF16 = jnp.bfloat16
F32 = jnp.float32
SMEM = pl.BlockSpec(memory_space=pltpu.SMEM)
WHOLE = pl.BlockSpec(memory_space=pltpu.VMEM)


COST = pl.CostEstimate(flops=1 << 20, bytes_accessed=1 << 16, transcendentals=0)


def three_terms(norm):
    high = norm.astype(BF16).astype(F32)
    middle = (norm - high).astype(BF16).astype(F32)
    return high, middle, norm - high - middle


def widened(rows, centre_side):
    wide = rows.astype(F32)
    high, middle, low = three_terms(jnp.sum(wide * wide, axis=1, keepdims=True))
    lane = lax.broadcasted_iota(jnp.int32, (rows.shape[0], 128), 1)
    first, ones = (3, 0) if centre_side else (0, 3)
    extra = jnp.where((lane >= ones) & (lane < ones + 3), 1.0, 0.0)
    extra = jnp.where(lane == first, high, extra)
    extra = jnp.where(lane == first + 1, middle, extra)
    extra = jnp.where(lane == first + 2, low, extra)
    own = (wide * -2.0).astype(BF16) if centre_side else rows
    return jnp.concatenate([own, extra.astype(BF16)], axis=1)


def in_vmem(*arrays):
    return [pltpu.with_memory_space_constraint(array, pltpu.VMEM) for array in arrays]


def kern_kernel(radius, parts, sides, place_ref, pattern_ref, *refs):
    queries, centres = refs[:parts], refs[parts:-3]
    kern_ref, query_wide, centre_wide = refs[-3:]
    me, core, mine = place_ref[0], place_ref[1], place_ref[2]
    side = 1 - 2 * lax.rem(me, 2)
    block_at = lambda steps: me + side * jnp.where(core == 0, steps[0], steps[1])

    rows = query_wide.shape[0] // parts
    for k, piece in enumerate(queries):
        at = pl.multiple_of((mine ^ k) * rows, rows) if parts > 1 else 0
        query_wide[pl.ds(at, rows), :] = widened(piece[...], False)

    depth = centre_wide.shape[0]
    band = pattern_ref.shape[1]
    query_block = jnp.clip(block_at(sides[0]), 0, pattern_ref.shape[0] - 1)
    tile = min(512, query_wide.shape[0])
    columns = min(256, depth)
    for b, (steps, centre) in enumerate(zip(sides[1:], centres)):
        centre_wide[...] = widened(centre[...], True)
        offset = jnp.clip(block_at(steps) - query_block + band // 2, 0, band - 1)
        cut = jnp.where(pattern_ref[query_block, offset] > 0, jnp.float32(radius), jnp.float32(-1.0))

        @pl.loop(0, query_wide.shape[0] // tile)
        def _(row):
            span = pl.ds(pl.multiple_of(row * tile, tile), tile)
            query = query_wide[span, :]
            for start in range(0, depth, columns):
                square = lax.dot_general(
                    query, centre_wide[pl.ds(start, columns), :], (((1,), (1,)), ((), ())), preferred_element_type=F32
                )
                square = jnp.maximum(square, 1e-30)
                dist = square * lax.rsqrt(square)
                inner = jnp.maximum(cut - dist, 0.0)
                inner = inner * inner
                kern_ref[span, pl.ds(b * depth + start, columns)] = (inner * inner * (dist + radius / 4)).astype(BF16)


def kern_blocks(place, pattern, queries, centres, sides):
    parts, blocks = len(queries), len(centres)
    features = queries[0].shape[1]
    query_rows, centre_rows = parts * queries[0].shape[0], centres[0].shape[0]
    return pl.pallas_call(
        functools.partial(kern_kernel, RADIUS_FACTOR * math.sqrt(features), parts, sides),
        in_specs=[SMEM, SMEM] + [WHOLE] * (parts + blocks),
        out_specs=WHOLE,
        out_shape=pltpu.VMEM((query_rows, blocks * centre_rows), BF16),
        scratch_shapes=[
            pltpu.VMEM((query_rows, features + 128), BF16),
            pltpu.VMEM((centre_rows, features + 128), BF16),
        ],
        compiler_params=pltpu.CompilerParams(vmem_limit_bytes=VMEM_LIMIT),
        cost_estimate=COST,
        name="kern",
    )(place, pattern, *queries, *centres)


def score_sum(terms, kern_refs, coef_refs, rows):
    total = None
    for kern, block, coef, column, width in terms:
        depth = coef_refs[coef].shape[0]
        product = jnp.dot(
            kern_refs[kern][rows, pl.ds(block * depth, depth)],
            coef_refs[coef][:, pl.ds(column, width)],
            preferred_element_type=F32,
        )
        total = product if total is None else total + product
    return total


def score_kernel(terms, kerns, tile, *refs):
    out_ref = refs[-1]

    @pl.loop(0, out_ref.shape[0] // tile)
    def _(row):
        rows = pl.ds(pl.multiple_of(row * tile, tile), tile)
        out_ref[rows, :] = score_sum(terms, refs[:kerns], refs[kerns:-1], rows).astype(out_ref.dtype)


def scores(kerns, coefs, terms, dtype):
    rows, width = kerns[0].shape[0], terms[0][4]
    return pl.pallas_call(
        functools.partial(score_kernel, terms, len(kerns), min(256, rows)),
        in_specs=[WHOLE] * (len(kerns) + len(coefs)),
        out_specs=WHOLE,
        out_shape=pltpu.VMEM((rows, width), dtype),
        compiler_params=pltpu.CompilerParams(vmem_limit_bytes=VMEM_LIMIT),
        cost_estimate=COST,
        name="scores",
    )(*in_vmem(*kerns, *coefs))


def final_kernel(terms, scale, tile, column, kern_ref, coef_ref, mid_ref, part_ref, *refs):
    out_ref = refs[-1]
    rows = pl.ds(pl.multiple_of(pl.program_id(0) * tile, tile), tile)
    total = score_sum(terms, [kern_ref], [coef_ref], rows) + part_ref[rows, :].astype(F32)
    total = total + mid_ref[rows, pl.ds(column, total.shape[1])]
    out_ref[...] = (total * scale).astype(out_ref.dtype)


def final(kern, coef, mid, part, scale, half, halves, out):
    rows, width = part.shape
    tile = min(256, rows)
    terms = ((0, 0, 0, 0, width),)
    return pl.pallas_call(
        functools.partial(final_kernel, terms, scale, tile, half * width),
        grid=(rows // tile,),
        in_specs=[WHOLE] * 4 + ([] if out is None else [pl.BlockSpec(memory_space=pl.ANY)]),
        out_specs=pl.BlockSpec((tile, width), lambda r: (r, half)),
        out_shape=jax.ShapeDtypeStruct((rows, width * halves), BF16),
        input_output_aliases={} if out is None else {4: 0},
        compiler_params=pltpu.CompilerParams(vmem_limit_bytes=VMEM_LIMIT),
        cost_estimate=COST,
        name="final",
    )(*in_vmem(kern, coef, mid, part), *([] if out is None else [out]))


def after(array, *others):
    return lax.optimization_barrier((array, *others))[0]


def per_device(queries, centres, coefs, pattern):
    blocks, members = lax.axis_size("pb"), lax.axis_size("ao")
    shares = members // 2
    radius = RADIUS_FACTOR * math.sqrt(queries.shape[1])
    me, member = lax.axis_index("pb"), lax.axis_index("ao")
    core, mine = lax.rem(member, 2), member // 2
    place = jnp.stack([me, core, mine])

    def send(block, *targets):
        route = []
        for i in range(blocks):
            for m in range(members):
                target = targets[m % 2](i)
                if target is not None and 0 <= target[0] < blocks:
                    route.append((i * members + m, target[0] * members + m // 2 * 2 + target[1]))
        return lax.ppermute(block, ("pb", "ao"), route)

    sign = lambda i: 1 - 2 * (i % 2)
    partner = lambda c: lambda i: (i + sign(i), c)
    front = lambda c: lambda i: (i + 2 * sign(i), c)
    back = lambda c: lambda i: (i - 2 * sign(i), c)
    nobody = lambda i: None

    def spread(piece):
        held, step = [piece], 1
        while step < shares:
            route = [(m, m ^ (2 * step)) for m in range(members)]
            held += [lax.ppermute(h, "ao", route) for h in held]
            step *= 2
        return held

    near = send(coefs, partner(0), back(1))
    query_rows = queries.shape[0] // shares
    query_part = lax.dynamic_slice_in_dim(queries, mine * query_rows, query_rows, 0)
    query_t = spread(send(query_part, back(0), partner(1)))
    far_1 = send(coefs, nobody, front(1))
    centre_own = lax.all_gather(centres, "ao", axis=0, tiled=True)
    centre_near = send(centre_own, back(1), partner(0))
    far_source = jnp.where(core == 0, centre_own, centre_near)
    centre_far = send(far_source, front(1), lambda i: (i, 0))

    kern_t = kern_blocks(place, pattern, query_t, [centre_own, centre_near], ((2, 1), (0, 0), (1, 2)))
    pattern_1 = after(pattern, kern_t)
    kern_m = kern_blocks(place, pattern_1, [queries], [centre_own, centre_near], ((0, 0), (0, 0), (1, 2)))
    kern_t = after(kern_t, kern_m)

    width = coefs.shape[1] // 2
    total, part = [], []
    for h in range(2):
        terms = ((0, 0, 0, h * width, width), (0, 1, 1, h * width, width))
        total.append(scores([kern_t], [coefs, near], terms, BF16))
        part.append(send(total[h], front(0), partner(1)))
    coefs_late = after(coefs, total[1])
    far_0 = [send(coefs_late[:, h * width : (h + 1) * width], back(0), nobody) for h in range(2)]
    pattern_2 = after(pattern, total[1])
    kern_far = kern_blocks(place, pattern_2, [queries], [centre_far], ((0, 0), (2, -2)))

    scale = 4.0 / radius**5
    whole = 2 * width
    mid = scores(
        [kern_m, kern_far], [coefs, near, far_1], ((0, 0, 0, 0, whole), (0, 1, 1, 0, whole), (1, 0, 2, 0, whole)), F32
    )
    out = None
    for h in range(2):
        out = final(kern_far, far_0[h], mid, part[h], scale, h, 2, out)
    return out


def solution(mesh):
    in_specs = (P("pb", None), P(("pb", "ao"), None), P("pb", "ao"), P())
    out_specs = P("pb", "ao")
    return jax.shard_map(
        per_device, mesh=mesh, in_specs=in_specs, out_specs=out_specs, check_vma=False
    )
```

```python
import functools
import math

import jax
import jax.numpy as jnp
from jax import lax
from jax.experimental import pallas as pl
from jax.experimental.pallas import tpu as pltpu
from jax.sharding import PartitionSpec as P

RADIUS_FACTOR = 1.3
VMEM_LIMIT = 24 * 1024 * 1024
BF16 = jnp.bfloat16
F32 = jnp.float32
SMEM = pl.BlockSpec(memory_space=pltpu.SMEM)
WHOLE = pl.BlockSpec(memory_space=pltpu.VMEM)


COST = pl.CostEstimate(flops=1 << 20, bytes_accessed=1 << 16, transcendentals=0)


def three_terms(norm):
    high = norm.astype(BF16).astype(F32)
    middle = (norm - high).astype(BF16).astype(F32)
    return high, middle, norm - high - middle


def widened(rows, centre_side):
    wide = rows.astype(F32)
    high, middle, low = three_terms(jnp.sum(wide * wide, axis=1, keepdims=True))
    lane = lax.broadcasted_iota(jnp.int32, (rows.shape[0], 128), 1)
    first, ones = (3, 0) if centre_side else (0, 3)
    extra = jnp.where((lane >= ones) & (lane < ones + 3), 1.0, 0.0)
    extra = jnp.where(lane == first, high, extra)
    extra = jnp.where(lane == first + 1, middle, extra)
    extra = jnp.where(lane == first + 2, low, extra)
    own = (wide * -2.0).astype(BF16) if centre_side else rows
    return jnp.concatenate([own, extra.astype(BF16)], axis=1)


def in_vmem(*arrays):
    return [pltpu.with_memory_space_constraint(array, pltpu.VMEM) for array in arrays]


def kern_tile(query, centre_wide, cut, radius, put):
    depth = centre_wide.shape[0]
    columns = min(256, depth)
    for start in range(0, depth, columns):
        span = pl.ds(start, columns)
        square = lax.dot_general(
            query, centre_wide[span, :], (((1,), (1,)), ((), ())), preferred_element_type=F32
        )
        square = jnp.maximum(square, 1e-30)
        dist = square * lax.rsqrt(square)
        inner = jnp.maximum(cut - dist, 0.0)
        inner = inner * inner
        put(span, (inner * inner * (dist + radius / 4)).astype(BF16))


def kern_kernel(radius, steps, sources, scored, carried, halves, place_ref, pattern_ref, query_ref, *refs):
    centre = refs[0][...]
    for source in refs[1:sources]:
        centre = centre + source[...]
    extra = refs[sources : sources + scored]
    first = sources + scored + carried
    out_ref, *half_refs = refs[first : first + 1 + halves]
    query_wide, centre_wide, *scratch = refs[first + 1 + halves :]
    copies = []
    if scored:
        kern_ref, coef_ref, sems = scratch
        copies.append(pltpu.make_async_copy(extra[0], coef_ref, sems.at[0]))
        for h, half_ref in enumerate(half_refs):
            columns = pl.ds(h * half_ref.shape[1], half_ref.shape[1])
            copies.append(pltpu.make_async_copy(refs[first - 1].at[:, columns], half_ref, sems.at[1 + h]))
    for copy in copies:
        copy.start()

    query_wide[...] = widened(query_ref[...], False)
    centre_wide[...] = widened(centre, True)
    me, core = place_ref[0], place_ref[1]
    side = 1 - 2 * lax.rem(me, 2)
    blocks, band = pattern_ref.shape
    query_block, centre_block = (me + side * jnp.where(core == 0, step[0], step[1]) for step in steps)
    query_block = jnp.clip(query_block, 0, blocks - 1)
    offset = jnp.clip(centre_block - query_block + band // 2, 0, band - 1)
    cut = jnp.where(pattern_ref[query_block, offset] > 0, jnp.float32(radius), jnp.float32(-1.0))

    tile = min(512, query_wide.shape[0])
    for row in range(query_wide.shape[0] // tile):
        rows = pl.ds(row * tile, tile)

        def put(span, value):
            if scored:
                kern_ref[:, span] = value
            else:
                out_ref[rows, span] = value

        kern_tile(query_wide[rows, :], centre_wide, cut, radius, put)
        if row == 0:
            for copy in copies:
                copy.wait()
        if scored:
            total = jnp.dot(kern_ref[...], coef_ref[...], preferred_element_type=F32)
            total = total + extra[1][rows, :].astype(F32) if scored == 2 else total
            out_ref[rows, :] = total.astype(out_ref.dtype)


def kern_blocks(place, pattern, queries, centres, steps, coefs=None, add=None, dtype=BF16, halves=0, carry=None):
    query_rows, features = queries.shape
    centre_rows = centres[0].shape[0]
    scratch = [
        pltpu.VMEM((query_rows, features + 128), BF16),
        pltpu.VMEM((centre_rows, features + 128), BF16),
    ]
    extra, specs, out_shape = [], [], pltpu.VMEM((query_rows, centre_rows), BF16)
    if coefs is not None:
        width = coefs.shape[1]
        extra, specs, out_shape = [coefs], [pl.BlockSpec(memory_space=pl.ANY)], pltpu.VMEM((query_rows, width), dtype)
        scratch += [
            pltpu.VMEM((min(512, query_rows), centre_rows), BF16),
            pltpu.VMEM(coefs.shape, BF16),
            pltpu.SemaphoreType.DMA((1 + halves,)),
        ]
        if halves:
            out_shape = [out_shape] + [pltpu.VMEM((centre_rows, carry.shape[1] // halves), BF16)] * halves
    if add is not None:
        extra, specs = extra + in_vmem(add), specs + [WHOLE]
    scored = len(extra)
    if carry is not None:
        extra, specs = extra + [carry], specs + [pl.BlockSpec(memory_space=pl.ANY)]
    return pl.pallas_call(
        functools.partial(
            kern_kernel, RADIUS_FACTOR * math.sqrt(features), steps, len(centres), scored, len(extra) - scored, halves
        ),
        in_specs=[SMEM, SMEM] + [WHOLE] * (1 + len(centres)) + specs,
        out_specs=[WHOLE] * (1 + halves) if halves else WHOLE,
        out_shape=out_shape,
        scratch_shapes=scratch,
        compiler_params=pltpu.CompilerParams(vmem_limit_bytes=VMEM_LIMIT),
        cost_estimate=COST,
        name="kern",
    )(place, pattern, queries, *centres, *extra)


def score_sum(terms, kern_refs, coef_refs, rows):
    total = None
    for kern, block, coef, column, width in terms:
        depth = coef_refs[coef].shape[0]
        product = jnp.dot(
            kern_refs[kern][rows, pl.ds(block * depth, depth)],
            coef_refs[coef][:, pl.ds(column, width)],
            preferred_element_type=F32,
        )
        total = product if total is None else total + product
    return total


def score_kernel(terms, kerns, adds, column, tile, *refs):
    out_ref = refs[-1]
    coefs = refs[kerns : len(refs) - 1 - adds]

    @pl.loop(0, out_ref.shape[0] // tile)
    def _(row):
        rows = pl.ds(pl.multiple_of(row * tile, tile), tile)
        total = score_sum(terms, refs[:kerns], coefs, rows)
        if adds:
            total = total + refs[-2][rows, pl.ds(column, total.shape[1])].astype(F32)
        out_ref[rows, :] = total.astype(out_ref.dtype)


def scores(kerns, coefs, terms, dtype, add=None, column=0):
    rows, width = kerns[0].shape[0], terms[0][4]
    adds = [] if add is None else [add]
    return pl.pallas_call(
        functools.partial(score_kernel, terms, len(kerns), len(adds), column, min(256, rows)),
        in_specs=[WHOLE] * (len(kerns) + len(coefs) + len(adds)),
        out_specs=WHOLE,
        out_shape=pltpu.VMEM((rows, width), dtype),
        compiler_params=pltpu.CompilerParams(vmem_limit_bytes=VMEM_LIMIT),
        cost_estimate=COST,
        name="scores",
    )(*in_vmem(*kerns, *coefs, *adds))


def final_kernel(scale, tile, column, place_ref, kern_ref, far_0_ref, far_1_ref, mid_ref, part_ref, *refs):
    out_ref = refs[-1]
    core = place_ref[1]
    rows = pl.ds(pl.multiple_of(pl.program_id(0) * tile, tile), tile)
    columns = pl.ds(column, out_ref.shape[1])

    def finish(coefs):
        total = jnp.dot(kern_ref[rows, :], coefs, preferred_element_type=F32)
        total = total + part_ref[rows, :].astype(F32) + mid_ref[rows, columns]
        out_ref[...] = (total * scale).astype(out_ref.dtype)

    @pl.when(core == 0)
    def _():
        finish(far_0_ref[...])

    @pl.when(core == 1)
    def _():
        finish(far_1_ref[:, columns])


def final(place, kern, far_0, far_1, mid, part, scale, half, halves, out):
    rows, width = part.shape
    tile = min(512, rows)
    return pl.pallas_call(
        functools.partial(final_kernel, scale, tile, half * width),
        grid=(rows // tile,),
        in_specs=[SMEM] + [WHOLE] * 5 + ([] if out is None else [pl.BlockSpec(memory_space=pl.ANY)]),
        out_specs=pl.BlockSpec((tile, width), lambda r: (r, half)),
        out_shape=jax.ShapeDtypeStruct((rows, width * halves), BF16),
        input_output_aliases={} if out is None else {6: 0},
        compiler_params=pltpu.CompilerParams(vmem_limit_bytes=VMEM_LIMIT),
        cost_estimate=COST,
        name="final",
    )(place, *in_vmem(kern, far_0, far_1, mid, part), *([] if out is None else [out]))


def after(array, *others):
    return lax.optimization_barrier((array, *others))[0]


def per_device(queries, centres, coefs, pattern):
    blocks, members = lax.axis_size("pb"), lax.axis_size("ao")
    radius = RADIUS_FACTOR * math.sqrt(queries.shape[1])
    me, core = lax.axis_index("pb"), lax.rem(lax.axis_index("ao"), 2)
    place = jnp.stack([me, core])

    def send(block, *targets):
        route = []
        for i in range(blocks):
            for m in range(members):
                target = targets[m % 2](i)
                if target is not None and 0 <= target[0] < blocks:
                    route.append((i * members + m, target[0] * members + m // 2 * 2 + target[1]))
        return lax.ppermute(block, ("pb", "ao"), route)

    sign = lambda i: 1 - 2 * (i % 2)
    partner = lambda c: lambda i: (i + sign(i), c)
    front = lambda c: lambda i: (i + 2 * sign(i), c)
    back = lambda c: lambda i: (i - 2 * sign(i), c)
    nobody = lambda i: None

    near = send(coefs, partner(0), back(1))
    query_t = send(queries, back(0), partner(1))
    far_1 = send(coefs, nobody, front(1))
    centre_own = lax.all_gather(centres, "ao", axis=0, tiled=True)
    centre_near = send(after(centre_own, query_t), back(1), partner(0))

    def kern(order, query_block, centre_block, query_at, centre_at, *scored):
        return kern_blocks(after(place, *order), pattern, query_block, centre_block, (query_at, centre_at), *scored)

    at_me, at_target, at_near, at_far = (0, 0), (2, 1), (1, 2), (2, -2)
    width = coefs.shape[1] // 2
    coefs_hbm = pltpu.with_memory_space_constraint(coefs, pltpu.HBM)
    base_t = kern((), query_t, [centre_own], at_target, at_me, coefs_hbm)
    base_m, *halves = kern((base_t,), queries, [centre_own], at_me, at_me, coefs_hbm, None, BF16, 2, coefs_hbm)
    kern_t = kern((base_m,), query_t, [centre_near], at_target, at_near)

    total, part = [], []
    for h in range(2):
        total.append(scores([kern_t], [near], ((0, 0, 0, h * width, width),), BF16, base_t, h * width))
        part.append(send(total[h], front(0), partner(1)))
    far_0 = [send(after(halves[0], kern_t), back(0), nobody), send(after(halves[1], total[0], far_1), back(0), nobody)]
    centre_far_0 = send(after(centre_near, total[1]), nobody, lambda i: (i, 0))
    centre_far_1 = send(after(centre_own, total[1]), nobody, front(1))
    mid, far_1 = kern((total[1],), queries, [centre_near], at_me, at_near, near, base_m, F32, 1, far_1)
    kern_far = kern((mid,), queries, [centre_far_0, centre_far_1], at_me, at_far)

    scale = 4.0 / radius**5
    out = None
    for h in range(2):
        out = final(place, kern_far, far_0[h], far_1, mid, part[h], scale, h, 2, out)
    return out


def solution(mesh):
    in_specs = (P("pb", None), P(("pb", "ao"), None), P("pb", "ao"), P())
    out_specs = P("pb", "ao")
    return jax.shard_map(
        per_device, mesh=mesh, in_specs=in_specs, out_specs=out_specs, check_vma=False
    )
```

```python
import functools
import math

import jax
import jax.numpy as jnp
from jax import lax
from jax.experimental import pallas as pl
from jax.experimental.pallas import tpu as pltpu
from jax.sharding import PartitionSpec as P

RADIUS_FACTOR = 1.3
VMEM_LIMIT = 24 * 1024 * 1024
BF16 = jnp.bfloat16
F32 = jnp.float32
SMEM = pl.BlockSpec(memory_space=pltpu.SMEM)
WHOLE = pl.BlockSpec(memory_space=pltpu.VMEM)
ANY = pl.BlockSpec(memory_space=pl.ANY)


COST = pl.CostEstimate(flops=1 << 20, bytes_accessed=1 << 16, transcendentals=0)


def three_terms(norm):
    high = norm.astype(BF16).astype(F32)
    middle = (norm - high).astype(BF16).astype(F32)
    return high, middle, norm - high - middle


def widened(rows, centre_side):
    wide = rows.astype(F32)
    high, middle, low = three_terms(jnp.sum(wide * wide, axis=1, keepdims=True))
    lane = lax.broadcasted_iota(jnp.int32, (rows.shape[0], 128), 1)
    first, ones = (3, 0) if centre_side else (0, 3)
    extra = jnp.where((lane >= ones) & (lane < ones + 3), 1.0, 0.0)
    extra = jnp.where(lane == first, high, extra)
    extra = jnp.where(lane == first + 1, middle, extra)
    extra = jnp.where(lane == first + 2, low, extra)
    own = (wide * -2.0).astype(BF16) if centre_side else rows
    return jnp.concatenate([own, extra.astype(BF16)], axis=1)


def in_vmem(*arrays):
    return [pltpu.with_memory_space_constraint(array, pltpu.VMEM) for array in arrays]


def kern_tile(query, centre_wide, cut, radius, out_ref, column):
    depth = centre_wide.shape[0]
    columns = min(256, depth)
    for start in range(0, depth, columns):
        square = lax.dot_general(
            query, centre_wide[pl.ds(start, columns), :], (((1,), (1,)), ((), ())), preferred_element_type=F32
        )
        square = jnp.maximum(square, 1e-30)
        dist = square * lax.rsqrt(square)
        inner = jnp.maximum(cut - dist, 0.0)
        inner = inner * inner
        out_ref[:, pl.ds(column + start, columns)] = (inner * inner * (dist + radius / 4)).astype(BF16)


def kern_kernel(radius, steps, sources, scored, carried, place_ref, pattern_ref, query_ref, *refs):
    blocks = len(steps) - 1
    centres, refs = refs[: blocks * sources], refs[blocks * sources :]
    coefs, refs = refs[: blocks * scored], refs[blocks * scored :]
    carry, refs = refs[:carried], refs[carried:]
    out_ref, *carry_out = refs[: 1 + carried]
    query_wide, centre_wide, *scratch = refs[1 + carried :]
    copies = []
    if scored:
        kern_ref, coef_ref, sems = scratch
        depth = centre_wide.shape[1]
        for b, coef in enumerate(coefs):
            copies.append(pltpu.make_async_copy(coef, coef_ref.at[pl.ds(b * depth, depth), :], sems.at[b]))
        for source, target in zip(carry, carry_out):
            copies.append(pltpu.make_async_copy(source, target, sems.at[blocks]))
    for copy in copies:
        copy.start()

    me, core = place_ref[0], place_ref[1]
    side = 1 - 2 * lax.rem(me, 2)
    listed, band = pattern_ref.shape
    query_block, *centre_blocks = (me + side * jnp.where(core == 0, step[0], step[1]) for step in steps)
    query_block = jnp.clip(query_block, 0, listed - 1)
    query_wide[...] = widened(query_ref[...], False)
    cuts = []
    for b, centre_block in enumerate(centre_blocks):
        centre = centres[b * sources][...]
        for source in centres[b * sources + 1 : (b + 1) * sources]:
            centre = centre + source[...]
        centre_wide[b] = widened(centre, True)
        offset = jnp.clip(centre_block - query_block + band // 2, 0, band - 1)
        cuts.append(jnp.where(pattern_ref[query_block, offset] > 0, jnp.float32(radius), jnp.float32(-1.0)))

    tile = min(512, query_wide.shape[0])
    for row in range(query_wide.shape[0] // tile):
        rows = pl.ds(row * tile, tile)
        values = kern_ref if scored else out_ref.at[rows, :]
        for b, cut in enumerate(cuts):
            kern_tile(query_wide[rows, :], centre_wide.at[b], cut, radius, values, b * centre_wide.shape[1])
        if row == 0:
            for copy in copies:
                copy.wait()
        if scored:
            total = jnp.dot(kern_ref[...], coef_ref[...], preferred_element_type=F32)
            out_ref[rows, :] = total.astype(out_ref.dtype)


def kern_blocks(place, pattern, queries, centres, steps, coefs=(), dtype=BF16, carry=()):
    query_rows, features = queries.shape
    blocks, centre_rows = len(centres), centres[0][0].shape[0]
    scratch = [
        pltpu.VMEM((query_rows, features + 128), BF16),
        pltpu.VMEM((blocks, centre_rows, features + 128), BF16),
    ]
    out_shape = [pltpu.VMEM((query_rows, blocks * centre_rows), BF16)]
    if coefs:
        width = coefs[0].shape[1]
        out_shape = [pltpu.VMEM((query_rows, width), dtype)]
        scratch += [
            pltpu.VMEM((min(512, query_rows), blocks * centre_rows), BF16),
            pltpu.VMEM((blocks * centre_rows, width), BF16),
            pltpu.SemaphoreType.DMA((blocks + 1,)),
        ]
    out_shape += [pltpu.VMEM(array.shape, array.dtype) for array in carry]
    pieces = [source for block in centres for source in block]
    out = pl.pallas_call(
        functools.partial(
            kern_kernel, RADIUS_FACTOR * math.sqrt(features), steps, len(centres[0]), len(coefs) > 0, len(carry)
        ),
        in_specs=[SMEM, SMEM] + [WHOLE] * (1 + len(pieces)) + [ANY] * (len(coefs) + len(carry)),
        out_specs=[WHOLE] * len(out_shape),
        out_shape=out_shape,
        scratch_shapes=scratch,
        compiler_params=pltpu.CompilerParams(vmem_limit_bytes=VMEM_LIMIT),
        cost_estimate=COST,
        name="kern",
    )(place, pattern, queries, *pieces, *coefs, *carry)
    return out if carry else out[0]


def score_sum(terms, kern_refs, coef_refs, rows):
    total = None
    for kern, block, coef, column, width in terms:
        depth = coef_refs[coef].shape[0]
        product = jnp.dot(
            kern_refs[kern][rows, pl.ds(block * depth, depth)],
            coef_refs[coef][:, pl.ds(column, width)],
            preferred_element_type=F32,
        )
        total = product if total is None else total + product
    return total


def score_kernel(terms, kerns, adds, column, tile, *refs):
    out_ref = refs[-1]
    coefs = refs[kerns : len(refs) - 1 - adds]

    @pl.loop(0, out_ref.shape[0] // tile)
    def _(row):
        rows = pl.ds(pl.multiple_of(row * tile, tile), tile)
        total = score_sum(terms, refs[:kerns], coefs, rows)
        if adds:
            total = total + refs[-2][rows, pl.ds(column, total.shape[1])].astype(F32)
        out_ref[rows, :] = total.astype(out_ref.dtype)


def scores(kerns, coefs, terms, dtype, add=None, column=0):
    rows, width = kerns[0].shape[0], terms[0][4]
    adds = [] if add is None else [add]
    return pl.pallas_call(
        functools.partial(score_kernel, terms, len(kerns), len(adds), column, min(256, rows)),
        in_specs=[WHOLE] * (len(kerns) + len(coefs) + len(adds)),
        out_specs=WHOLE,
        out_shape=pltpu.VMEM((rows, width), dtype),
        compiler_params=pltpu.CompilerParams(vmem_limit_bytes=VMEM_LIMIT),
        cost_estimate=COST,
        name="scores",
    )(*in_vmem(*kerns, *coefs, *adds))


def far_kernel(tile, place_ref, kern_ref, far_0_ref, far_1_ref, add_ref, out_ref):
    def sums(coef_ref):
        @pl.loop(0, out_ref.shape[0] // tile)
        def _(row):
            rows = pl.ds(pl.multiple_of(row * tile, tile), tile)
            total = jnp.dot(kern_ref[rows, :], coef_ref[...], preferred_element_type=F32)
            out_ref[rows, :] = total + add_ref[rows, :]

    @pl.when(place_ref[1] == 0)
    def _():
        sums(far_0_ref)

    @pl.when(place_ref[1] == 1)
    def _():
        sums(far_1_ref)


def far_sum(place, kern, far_0, far_1, add):
    rows = kern.shape[0]
    return pl.pallas_call(
        functools.partial(far_kernel, min(256, rows)),
        in_specs=[SMEM] + [WHOLE] * 4,
        out_specs=WHOLE,
        out_shape=pltpu.VMEM(add.shape, add.dtype),
        input_output_aliases={4: 0},
        compiler_params=pltpu.CompilerParams(vmem_limit_bytes=VMEM_LIMIT),
        cost_estimate=COST,
        name="far",
    )(place, *in_vmem(kern, far_0, far_1, add))


def final_kernel(scale, tile, column, add_ref, part_ref, *refs):
    out_ref = refs[-1]
    rows = pl.ds(pl.multiple_of(pl.program_id(0) * tile, tile), tile)
    total = part_ref[rows, :].astype(F32) + add_ref[rows, pl.ds(column, out_ref.shape[1])]
    out_ref[...] = (total * scale).astype(out_ref.dtype)


def final(add, part, scale, half, halves, out):
    rows, width = part.shape
    tile = min(512, rows)
    return pl.pallas_call(
        functools.partial(final_kernel, scale, tile, half * width),
        grid=(rows // tile,),
        in_specs=[WHOLE] * 2 + ([] if out is None else [ANY]),
        out_specs=pl.BlockSpec((tile, width), lambda r: (r, half)),
        out_shape=jax.ShapeDtypeStruct((rows, width * halves), BF16),
        input_output_aliases={} if out is None else {2: 0},
        compiler_params=pltpu.CompilerParams(vmem_limit_bytes=VMEM_LIMIT),
        cost_estimate=COST,
        name="final",
    )(*in_vmem(add, part), *([] if out is None else [out]))


def after(array, *others):
    return lax.optimization_barrier((array, *others))[0]


def per_device(queries, centres, coefs, pattern):
    blocks, members = lax.axis_size("pb"), lax.axis_size("ao")
    radius = RADIUS_FACTOR * math.sqrt(queries.shape[1])
    me, core = lax.axis_index("pb"), lax.rem(lax.axis_index("ao"), 2)
    place = jnp.stack([me, core])

    def send(block, *targets):
        route = []
        for i in range(blocks):
            for m in range(members):
                target = targets[m % 2](i)
                if target is not None and 0 <= target[0] < blocks:
                    route.append((i * members + m, target[0] * members + m // 2 * 2 + target[1]))
        return lax.ppermute(block, ("pb", "ao"), route)

    sign = lambda i: 1 - 2 * (i % 2)
    partner = lambda c: lambda i: (i + sign(i), c)
    front = lambda c: lambda i: (i + 2 * sign(i), c)
    back = lambda c: lambda i: (i - 2 * sign(i), c)
    nobody = lambda i: None

    near = send(coefs, partner(0), back(1))
    query_t = send(queries, back(0), partner(1))
    far_1 = send(coefs, nobody, front(1))
    centre_own = lax.all_gather(centres, "ao", axis=0, tiled=True)
    centre_near = send(after(centre_own, query_t), back(1), partner(0))

    def kern(order, query_block, query_at, centre_blocks, at, *scored):
        return kern_blocks(after(place, *order), pattern, query_block, centre_blocks, (query_at, *at), *scored)

    at_me, at_target, at_near, at_far = (0, 0), (2, 1), (1, 2), (2, -2)
    width = coefs.shape[1] // 2
    coefs_hbm = pltpu.with_memory_space_constraint(coefs, pltpu.HBM)
    base_t = kern((), query_t, at_target, [[centre_own]], [at_me], [coefs_hbm])
    centre_far_1 = send(after(centre_own, base_t), nobody, front(1))
    kern_t = kern((base_t,), query_t, at_target, [[centre_near]], [at_near])
    far_0 = send(after(coefs, kern_t), back(0), nobody)
    near = after(near, kern_t)
    total, part = [], []
    for h in range(2):
        if h == 1:
            near = after(near, total[0], far_1, centre_far_1)
        total.append(scores([kern_t], [near], ((0, 0, 0, h * width, width),), BF16, base_t, h * width))
        part.append(send(total[h], front(0), partner(1)))
    centre_far_0 = send(after(centre_near, total[1]), nobody, lambda i: (i, 0))
    own, far_1 = kern(
        (total[1],), queries, at_me, [[centre_own], [centre_near]], [at_me, at_near], [coefs_hbm, near], F32, [far_1]
    )
    kern_far = kern((own,), queries, at_me, [[centre_far_0, centre_far_1]], [at_far])
    own = far_sum(place, kern_far, far_0, far_1, own)

    scale = 4.0 / radius**5
    out = None
    for h in range(2):
        out = final(own, part[h], scale, h, 2, out)
    return out


def solution(mesh):
    in_specs = (P("pb", None), P(("pb", "ao"), None), P("pb", "ao"), P())
    out_specs = P("pb", "ao")
    return jax.shard_map(
        per_device, mesh=mesh, in_specs=in_specs, out_specs=out_specs, check_vma=False
    )
```

```python
import functools
import math

import jax
import jax.numpy as jnp
from jax import lax
from jax.experimental import pallas as pl
from jax.experimental.pallas import tpu as pltpu
from jax.sharding import PartitionSpec as P

RADIUS_FACTOR = 1.3
VMEM_LIMIT = 24 * 1024 * 1024
BF16 = jnp.bfloat16
F32 = jnp.float32
SMEM = pl.BlockSpec(memory_space=pltpu.SMEM)
WHOLE = pl.BlockSpec(memory_space=pltpu.VMEM)
ANY = pl.BlockSpec(memory_space=pl.ANY)


COST = pl.CostEstimate(flops=1 << 20, bytes_accessed=1 << 16, transcendentals=0)


def three_terms(norm):
    high = norm.astype(BF16).astype(F32)
    middle = (norm - high).astype(BF16).astype(F32)
    return high, middle, norm - high - middle


def widened(rows, centre_side):
    wide = rows.astype(F32)
    high, middle, low = three_terms(jnp.sum(wide * wide, axis=1, keepdims=True))
    lane = lax.broadcasted_iota(jnp.int32, (rows.shape[0], 128), 1)
    first, ones = (3, 0) if centre_side else (0, 3)
    extra = jnp.where((lane >= ones) & (lane < ones + 3), 1.0, 0.0)
    extra = jnp.where(lane == first, high, extra)
    extra = jnp.where(lane == first + 1, middle, extra)
    extra = jnp.where(lane == first + 2, low, extra)
    own = (wide * -2.0).astype(BF16) if centre_side else rows
    return jnp.concatenate([own, extra.astype(BF16)], axis=1)


def in_vmem(*arrays):
    return [pltpu.with_memory_space_constraint(array, pltpu.VMEM) for array in arrays]


def cut_kernel(radius, pairs, place_ref, pattern_ref, out_ref):
    me, core = place_ref[0], place_ref[1]
    side = 1 - 2 * lax.rem(me, 2)
    blocks, band = pattern_ref.shape
    for k, pair in enumerate(pairs):
        query_block, centre_block = (me + side * jnp.where(core == 0, step[0], step[1]) for step in pair)
        query_block = jnp.clip(query_block, 0, blocks - 1)
        offset = jnp.clip(centre_block - query_block + band // 2, 0, band - 1)
        cut = jnp.where(pattern_ref[query_block, offset] > 0, jnp.float32(radius), jnp.float32(-1.0))
        out_ref[k] = jnp.full(out_ref.shape[1:], cut, F32)


def cut_values(place, pattern, pairs, radius):
    return pl.pallas_call(
        functools.partial(cut_kernel, radius, pairs),
        in_specs=[SMEM, SMEM],
        out_specs=WHOLE,
        out_shape=pltpu.VMEM((len(pairs), 8, 256), F32),
        compiler_params=pltpu.CompilerParams(vmem_limit_bytes=VMEM_LIMIT),
        cost_estimate=COST,
        name="cuts",
    )(place, pattern)


def kern_tile(query, centre_wide, cut_ref, radius, out_ref, column):
    depth = centre_wide.shape[0]
    columns = min(256, depth)
    for start in range(0, depth, columns):
        square = lax.dot_general(
            query, centre_wide[pl.ds(start, columns), :], (((1,), (1,)), ((), ())), preferred_element_type=F32
        )
        square = jnp.maximum(square, 1e-30)
        dist = square * lax.rsqrt(square)
        inner = jnp.maximum(cut_ref[:1, :columns] - dist, 0.0)
        inner = inner * inner
        out_ref[:, pl.ds(column + start, columns)] = (inner * inner * (dist + radius / 4)).astype(BF16)


def kern_kernel(radius, cuts, sources, scored, carried, cut_ref, query_ref, *refs):
    blocks = len(cuts)
    centres, refs = refs[: blocks * sources], refs[blocks * sources :]
    coefs, refs = refs[: blocks * scored], refs[blocks * scored :]
    carry, refs = refs[:carried], refs[carried:]
    out_ref, *carry_out = refs[: 1 + carried]
    query_wide, centre_wide, *scratch = refs[1 + carried :]
    copies = []
    if scored:
        kern_ref, coef_ref, sems = scratch
        depth = centre_wide.shape[1]
        for b, coef in enumerate(coefs):
            copies.append(pltpu.make_async_copy(coef, coef_ref.at[pl.ds(b * depth, depth), :], sems.at[b]))
        for source, target in zip(carry, carry_out):
            copies.append(pltpu.make_async_copy(source, target, sems.at[blocks]))
    for copy in copies:
        copy.start()

    query_wide[...] = widened(query_ref[...], False)
    for b in range(blocks):
        centre = centres[b * sources][...]
        for source in centres[b * sources + 1 : (b + 1) * sources]:
            centre = centre + source[...]
        centre_wide[b] = widened(centre, True)

    tile = min(512, query_wide.shape[0])
    for row in range(query_wide.shape[0] // tile):
        rows = pl.ds(row * tile, tile)
        values = kern_ref if scored else out_ref.at[rows, :]
        for b, cut in enumerate(cuts):
            kern_tile(query_wide[rows, :], centre_wide.at[b], cut_ref.at[cut], radius, values, b * centre_wide.shape[1])
        if row == 0:
            for copy in copies:
                copy.wait()
        if scored:
            total = jnp.dot(kern_ref[...], coef_ref[...], preferred_element_type=F32)
            out_ref[rows, :] = total.astype(out_ref.dtype)


def kern_blocks(cut_rows, queries, centres, cuts, coefs=(), dtype=BF16, carry=()):
    query_rows, features = queries.shape
    blocks, centre_rows = len(centres), centres[0][0].shape[0]
    scratch = [
        pltpu.VMEM((query_rows, features + 128), BF16),
        pltpu.VMEM((blocks, centre_rows, features + 128), BF16),
    ]
    out_shape = [pltpu.VMEM((query_rows, blocks * centre_rows), BF16)]
    if coefs:
        width = coefs[0].shape[1]
        out_shape = [pltpu.VMEM((query_rows, width), dtype)]
        scratch += [
            pltpu.VMEM((min(512, query_rows), blocks * centre_rows), BF16),
            pltpu.VMEM((blocks * centre_rows, width), BF16),
            pltpu.SemaphoreType.DMA((blocks + 1,)),
        ]
    out_shape += [pltpu.VMEM(array.shape, array.dtype) for array in carry]
    pieces = [source for block in centres for source in block]
    out = pl.pallas_call(
        functools.partial(
            kern_kernel, RADIUS_FACTOR * math.sqrt(features), cuts, len(centres[0]), len(coefs) > 0, len(carry)
        ),
        in_specs=[WHOLE] * (2 + len(pieces)) + [ANY] * (len(coefs) + len(carry)),
        out_specs=[WHOLE] * len(out_shape),
        out_shape=out_shape,
        scratch_shapes=scratch,
        compiler_params=pltpu.CompilerParams(vmem_limit_bytes=VMEM_LIMIT),
        cost_estimate=COST,
        name="kern",
    )(cut_rows, queries, *pieces, *coefs, *carry)
    return out if carry else out[0]


def score_sum(terms, kern_refs, coef_refs, rows):
    total = None
    for kern, block, coef, column, width in terms:
        depth = coef_refs[coef].shape[0]
        product = jnp.dot(
            kern_refs[kern][rows, pl.ds(block * depth, depth)],
            coef_refs[coef][:, pl.ds(column, width)],
            preferred_element_type=F32,
        )
        total = product if total is None else total + product
    return total


def score_kernel(terms, kerns, adds, column, tile, *refs):
    out_ref = refs[-1]
    coefs = refs[kerns : len(refs) - 1 - adds]

    @pl.loop(0, out_ref.shape[0] // tile)
    def _(row):
        rows = pl.ds(pl.multiple_of(row * tile, tile), tile)
        total = score_sum(terms, refs[:kerns], coefs, rows)
        if adds:
            total = total + refs[-2][rows, pl.ds(column, total.shape[1])].astype(F32)
        out_ref[rows, :] = total.astype(out_ref.dtype)


def scores(kerns, coefs, terms, dtype, add=None, column=0):
    rows, width = kerns[0].shape[0], terms[0][4]
    adds = [] if add is None else [add]
    return pl.pallas_call(
        functools.partial(score_kernel, terms, len(kerns), len(adds), column, min(256, rows)),
        in_specs=[WHOLE] * (len(kerns) + len(coefs) + len(adds)),
        out_specs=WHOLE,
        out_shape=pltpu.VMEM((rows, width), dtype),
        compiler_params=pltpu.CompilerParams(vmem_limit_bytes=VMEM_LIMIT),
        cost_estimate=COST,
        name="scores",
    )(*in_vmem(*kerns, *coefs, *adds))


def far_kernel(tile, place_ref, kern_ref, far_0_ref, far_1_ref, add_ref, out_ref):
    def sums(coef_ref):
        @pl.loop(0, out_ref.shape[0] // tile)
        def _(row):
            rows = pl.ds(pl.multiple_of(row * tile, tile), tile)
            total = jnp.dot(kern_ref[rows, :], coef_ref[...], preferred_element_type=F32)
            out_ref[rows, :] = total + add_ref[rows, :]

    @pl.when(place_ref[1] == 0)
    def _():
        sums(far_0_ref)

    @pl.when(place_ref[1] == 1)
    def _():
        sums(far_1_ref)


def far_sum(place, kern, far_0, far_1, add):
    rows = kern.shape[0]
    return pl.pallas_call(
        functools.partial(far_kernel, min(256, rows)),
        in_specs=[SMEM] + [WHOLE] * 4,
        out_specs=WHOLE,
        out_shape=pltpu.VMEM(add.shape, add.dtype),
        input_output_aliases={4: 0},
        compiler_params=pltpu.CompilerParams(vmem_limit_bytes=VMEM_LIMIT),
        cost_estimate=COST,
        name="far",
    )(place, *in_vmem(kern, far_0, far_1, add))


def final_kernel(scale, tile, column, add_ref, part_ref, *refs):
    out_ref = refs[-1]
    rows = pl.ds(pl.multiple_of(pl.program_id(0) * tile, tile), tile)
    total = part_ref[rows, :].astype(F32) + add_ref[rows, pl.ds(column, out_ref.shape[1])]
    out_ref[...] = (total * scale).astype(out_ref.dtype)


def final(add, part, scale, half, halves, out):
    rows, width = part.shape
    tile = min(512, rows)
    return pl.pallas_call(
        functools.partial(final_kernel, scale, tile, half * width),
        grid=(rows // tile,),
        in_specs=[WHOLE] * 2 + ([] if out is None else [ANY]),
        out_specs=pl.BlockSpec((tile, width), lambda r: (r, half)),
        out_shape=jax.ShapeDtypeStruct((rows, width * halves), BF16),
        input_output_aliases={} if out is None else {2: 0},
        compiler_params=pltpu.CompilerParams(vmem_limit_bytes=VMEM_LIMIT),
        cost_estimate=COST,
        name="final",
    )(*in_vmem(add, part), *([] if out is None else [out]))


def after(array, *others):
    return lax.optimization_barrier((array, *others))[0]


def per_device(queries, centres, coefs, pattern):
    blocks, members = lax.axis_size("pb"), lax.axis_size("ao")
    radius = RADIUS_FACTOR * math.sqrt(queries.shape[1])
    me, core = lax.axis_index("pb"), lax.rem(lax.axis_index("ao"), 2)
    place = jnp.stack([me, core])

    def send(block, *targets):
        route = []
        for i in range(blocks):
            for m in range(members):
                target = targets[m % 2](i)
                if target is not None and 0 <= target[0] < blocks:
                    route.append((i * members + m, target[0] * members + m // 2 * 2 + target[1]))
        return lax.ppermute(block, ("pb", "ao"), route)

    sign = lambda i: 1 - 2 * (i % 2)
    partner = lambda c: lambda i: (i + sign(i), c)
    front = lambda c: lambda i: (i + 2 * sign(i), c)
    back = lambda c: lambda i: (i - 2 * sign(i), c)
    nobody = lambda i: None

    near = send(coefs, partner(0), back(1))
    query_t = send(queries, back(0), partner(1))
    far_1 = send(coefs, nobody, front(1))
    centre_own = lax.all_gather(centres, "ao", axis=0, tiled=True)
    centre_near = send(after(centre_own, query_t), back(1), partner(0))

    at_me, at_target, at_near, at_far = (0, 0), (2, 1), (1, 2), (2, -2)
    pairs = ((at_target, at_me), (at_target, at_near), (at_me, at_me), (at_me, at_near), (at_me, at_far))
    cut_rows = cut_values(place, pattern, pairs, radius)

    def kern(order, queries, query_at, centres, at, *scored):
        cuts = tuple(pairs.index((query_at, centre_at)) for centre_at in at)
        return kern_blocks(after(cut_rows, *order), queries, centres, cuts, *scored)

    width = coefs.shape[1] // 2
    coefs_hbm = pltpu.with_memory_space_constraint(coefs, pltpu.HBM)
    base_t = kern((), query_t, at_target, [[centre_own]], [at_me], [coefs_hbm])
    centre_far_1 = send(after(centre_own, base_t), nobody, front(1))
    kern_t = kern((base_t,), query_t, at_target, [[centre_near]], [at_near])
    far_0 = send(after(coefs, kern_t), back(0), nobody)
    near = after(near, kern_t)
    total, part = [], []
    for h in range(2):
        if h == 1:
            near = after(near, total[0], far_1, centre_far_1)
        total.append(scores([kern_t], [near], ((0, 0, 0, h * width, width),), BF16, base_t, h * width))
        part.append(send(total[h], front(0), partner(1)))
    centre_far_0 = send(after(centre_near, total[1]), nobody, lambda i: (i, 0))
    own, far_1 = kern(
        (total[1],), queries, at_me, [[centre_own], [centre_near]], [at_me, at_near], [coefs_hbm, near], F32, [far_1]
    )
    kern_far = kern((own,), queries, at_me, [[centre_far_0, centre_far_1]], [at_far])
    own = far_sum(place, kern_far, far_0, far_1, own)

    scale = 4.0 / radius**5
    out = None
    for h in range(2):
        out = final(own, part[h], scale, h, 2, out)
    return out


def solution(mesh):
    in_specs = (P("pb", None), P(("pb", "ao"), None), P("pb", "ao"), P())
    out_specs = P("pb", "ao")
    return jax.shard_map(
        per_device, mesh=mesh, in_specs=in_specs, out_specs=out_specs, check_vma=False
    )
```

```python
import functools
import math

import jax
import jax.numpy as jnp
from jax import lax
from jax.experimental import pallas as pl
from jax.experimental.pallas import tpu as pltpu
from jax.sharding import PartitionSpec as P

RADIUS_FACTOR = 1.3
VMEM_LIMIT = 24 * 1024 * 1024
BF16 = jnp.bfloat16
F32 = jnp.float32
SMEM = pl.BlockSpec(memory_space=pltpu.SMEM)
WHOLE = pl.BlockSpec(memory_space=pltpu.VMEM)
ANY = pl.BlockSpec(memory_space=pl.ANY)


COST = pl.CostEstimate(flops=1 << 20, bytes_accessed=1 << 16, transcendentals=0)


def three_terms(norm):
    high = norm.astype(BF16).astype(F32)
    middle = (norm - high).astype(BF16).astype(F32)
    return high, middle, norm - high - middle


def widened(rows, centre_side):
    wide = rows.astype(F32)
    high, middle, low = three_terms(jnp.sum(wide * wide, axis=1, keepdims=True))
    lane = lax.broadcasted_iota(jnp.int32, (rows.shape[0], 128), 1)
    first, ones = (3, 0) if centre_side else (0, 3)
    extra = jnp.where((lane >= ones) & (lane < ones + 3), 1.0, 0.0)
    extra = jnp.where(lane == first, high, extra)
    extra = jnp.where(lane == first + 1, middle, extra)
    extra = jnp.where(lane == first + 2, low, extra)
    own = (wide * -2.0).astype(BF16) if centre_side else rows
    return jnp.concatenate([own, extra.astype(BF16)], axis=1)


def in_vmem(*arrays):
    return [pltpu.with_memory_space_constraint(array, pltpu.VMEM) for array in arrays]


def cut_kernel(radius, pairs, place_ref, pattern_ref, out_ref):
    me, core = place_ref[0], place_ref[1]
    side = 1 - 2 * lax.rem(me, 2)
    blocks, band = pattern_ref.shape
    for k, pair in enumerate(pairs):
        query_block, centre_block = (me + side * jnp.where(core == 0, step[0], step[1]) for step in pair)
        query_block = jnp.clip(query_block, 0, blocks - 1)
        offset = jnp.clip(centre_block - query_block + band // 2, 0, band - 1)
        cut = jnp.where(pattern_ref[query_block, offset] > 0, jnp.float32(radius), jnp.float32(-1.0))
        out_ref[k] = jnp.full(out_ref.shape[1:], cut, F32)


def cut_values(place, pattern, pairs, radius):
    return pl.pallas_call(
        functools.partial(cut_kernel, radius, pairs),
        in_specs=[SMEM, SMEM],
        out_specs=WHOLE,
        out_shape=pltpu.VMEM((len(pairs), 8, 256), F32),
        compiler_params=pltpu.CompilerParams(vmem_limit_bytes=VMEM_LIMIT),
        cost_estimate=COST,
        name="cuts",
    )(place, pattern)


def kern_tile(query, centre_wide, cut_ref, radius, out_ref, column):
    depth = centre_wide.shape[0]
    columns = min(256, depth)
    for start in range(0, depth, columns):
        square = lax.dot_general(
            query, centre_wide[pl.ds(start, columns), :], (((1,), (1,)), ((), ())), preferred_element_type=F32
        )
        square = jnp.maximum(square, 1e-30)
        dist = square * lax.rsqrt(square)
        inner = jnp.maximum(cut_ref[:1, :columns] - dist, 0.0)
        inner = inner * inner
        out_ref[:, pl.ds(column + start, columns)] = (inner * inner * (dist + radius / 4)).astype(BF16)


def kern_kernel(radius, cuts, sources, scored, carried, cut_ref, query_ref, *refs):
    blocks = len(cuts)
    centres, refs = refs[: blocks * sources], refs[blocks * sources :]
    coefs, refs = refs[: blocks * scored], refs[blocks * scored :]
    carry, refs = refs[:carried], refs[carried:]
    out_ref, *carry_out = refs[: 1 + carried]
    query_wide, centre_wide, *scratch = refs[1 + carried :]
    copies = []
    if scored:
        kern_ref, coef_ref, sems = scratch
        depth = centre_wide.shape[1]
        for b, coef in enumerate(coefs):
            copies.append(pltpu.make_async_copy(coef, coef_ref.at[pl.ds(b * depth, depth), :], sems.at[b]))
        for source, target in zip(carry, carry_out):
            copies.append(pltpu.make_async_copy(source, target, sems.at[blocks]))
    for copy in copies:
        copy.start()

    query_wide[...] = widened(query_ref[...], False)
    for b in range(blocks):
        centre = centres[b * sources][...]
        for source in centres[b * sources + 1 : (b + 1) * sources]:
            centre = centre + source[...]
        centre_wide[b] = widened(centre, True)

    tile = min(512, query_wide.shape[0])
    for row in range(query_wide.shape[0] // tile):
        rows = pl.ds(row * tile, tile)
        values = kern_ref if scored else out_ref.at[rows, :]
        for b, cut in enumerate(cuts):
            kern_tile(query_wide[rows, :], centre_wide.at[b], cut_ref.at[cut], radius, values, b * centre_wide.shape[1])
        if row == 0:
            for copy in copies:
                copy.wait()
        if scored:
            total = jnp.dot(kern_ref[...], coef_ref[...], preferred_element_type=F32)
            out_ref[rows, :] = total.astype(out_ref.dtype)


def kern_blocks(cut_rows, queries, centres, cuts, coefs=(), dtype=BF16, carry=()):
    query_rows, features = queries.shape
    blocks, centre_rows = len(centres), centres[0][0].shape[0]
    scratch = [
        pltpu.VMEM((query_rows, features + 128), BF16),
        pltpu.VMEM((blocks, centre_rows, features + 128), BF16),
    ]
    out_shape = [pltpu.VMEM((query_rows, blocks * centre_rows), BF16)]
    if coefs:
        width = coefs[0].shape[1]
        out_shape = [pltpu.VMEM((query_rows, width), dtype)]
        scratch += [
            pltpu.VMEM((min(512, query_rows), blocks * centre_rows), BF16),
            pltpu.VMEM((blocks * centre_rows, width), BF16),
            pltpu.SemaphoreType.DMA((blocks + 1,)),
        ]
    out_shape += [pltpu.VMEM(array.shape, array.dtype) for array in carry]
    pieces = [source for block in centres for source in block]
    out = pl.pallas_call(
        functools.partial(
            kern_kernel, RADIUS_FACTOR * math.sqrt(features), cuts, len(centres[0]), len(coefs) > 0, len(carry)
        ),
        in_specs=[WHOLE] * (2 + len(pieces)) + [ANY] * (len(coefs) + len(carry)),
        out_specs=[WHOLE] * len(out_shape),
        out_shape=out_shape,
        scratch_shapes=scratch,
        compiler_params=pltpu.CompilerParams(vmem_limit_bytes=VMEM_LIMIT),
        cost_estimate=COST,
        name="kern",
    )(cut_rows, queries, *pieces, *coefs, *carry)
    return out if carry else out[0]


def score_sum(terms, kern_refs, coef_refs, rows):
    total = None
    for kern, block, coef, column, width in terms:
        depth = coef_refs[coef].shape[0]
        product = jnp.dot(
            kern_refs[kern][rows, pl.ds(block * depth, depth)],
            coef_refs[coef][:, pl.ds(column, width)],
            preferred_element_type=F32,
        )
        total = product if total is None else total + product
    return total


def score_kernel(terms, kerns, adds, column, tile, *refs):
    out_ref = refs[-1]
    coefs = refs[kerns : len(refs) - 1 - adds]

    for row in range(out_ref.shape[0] // tile):
        rows = pl.ds(row * tile, tile)
        total = score_sum(terms, refs[:kerns], coefs, rows)
        if adds:
            total = total + refs[-2][rows, pl.ds(column, total.shape[1])].astype(F32)
        out_ref[rows, :] = total.astype(out_ref.dtype)


def scores(kerns, coefs, terms, dtype, add=None, column=0):
    rows, width = kerns[0].shape[0], terms[0][4]
    adds = [] if add is None else [add]
    return pl.pallas_call(
        functools.partial(score_kernel, terms, len(kerns), len(adds), column, min(512, rows)),
        in_specs=[WHOLE] * (len(kerns) + len(coefs) + len(adds)),
        out_specs=WHOLE,
        out_shape=pltpu.VMEM((rows, width), dtype),
        compiler_params=pltpu.CompilerParams(vmem_limit_bytes=VMEM_LIMIT),
        cost_estimate=COST,
        name="scores",
    )(*in_vmem(*kerns, *coefs, *adds))


def far_kernel(
    scale, place_ref, kern_ref, far_0_ref, far_1_ref, add_ref, part_ref, out_ref, rest_ref, low_ref, sems
):
    width = part_ref.shape[1]
    tile = min(512, kern_ref.shape[0])
    tiles = [pl.ds(row * tile, tile) for row in range(kern_ref.shape[0] // tile)]
    low, high = pl.ds(0, width), pl.ds(width, width)

    def sums(coef_ref):
        copies = []
        for k, rows in enumerate(tiles):
            total = jnp.dot(kern_ref[rows, :], coef_ref[:, low], preferred_element_type=F32)
            total = total + add_ref[rows, low] + part_ref[rows, :].astype(F32)
            low_ref[rows, :] = (total * scale).astype(low_ref.dtype)
            copies.append(pltpu.make_async_copy(low_ref.at[rows, :], out_ref.at[rows, low], sems.at[k]))
            copies[k].start()
        for rows in tiles:
            total = jnp.dot(kern_ref[rows, :], coef_ref[:, high], preferred_element_type=F32)
            rest_ref[rows, :] = total + add_ref[rows, high]
        for copy in copies:
            copy.wait()

    @pl.when(place_ref[1] == 0)
    def _():
        sums(far_0_ref)

    @pl.when(place_ref[1] == 1)
    def _():
        sums(far_1_ref)


def far_sum(place, kern, far_0, far_1, add, part, scale):
    rows, width = part.shape
    return pl.pallas_call(
        functools.partial(far_kernel, scale),
        in_specs=[SMEM] + [WHOLE] * 5,
        out_specs=[ANY, WHOLE],
        out_shape=[jax.ShapeDtypeStruct(add.shape, BF16), pltpu.VMEM((rows, width), F32)],
        scratch_shapes=[
            pltpu.VMEM((rows, width), BF16),
            pltpu.SemaphoreType.DMA((rows // min(512, rows),)),
        ],
        compiler_params=pltpu.CompilerParams(vmem_limit_bytes=VMEM_LIMIT),
        cost_estimate=COST,
        name="far",
    )(place, *in_vmem(kern, far_0, far_1, add, part))


def final_kernel(scale, tile, add_ref, part_ref, _, out_ref):
    rows = pl.ds(pl.multiple_of(pl.program_id(0) * tile, tile), tile)
    total = part_ref[rows, :].astype(F32) + add_ref[rows, :]
    out_ref[...] = (total * scale).astype(out_ref.dtype)


def final(add, part, scale, out):
    rows, width = part.shape
    tile = min(512, rows)
    return pl.pallas_call(
        functools.partial(final_kernel, scale, tile),
        grid=(rows // tile,),
        in_specs=[WHOLE, WHOLE, ANY],
        out_specs=pl.BlockSpec((tile, width), lambda r: (r, 1)),
        out_shape=jax.ShapeDtypeStruct(out.shape, out.dtype),
        input_output_aliases={2: 0},
        compiler_params=pltpu.CompilerParams(vmem_limit_bytes=VMEM_LIMIT),
        cost_estimate=COST,
        name="final",
    )(*in_vmem(add, part), out)


def after(array, *others):
    return lax.optimization_barrier((array, *others))[0]


def per_device(queries, centres, coefs, pattern):
    blocks, members = lax.axis_size("pb"), lax.axis_size("ao")
    radius = RADIUS_FACTOR * math.sqrt(queries.shape[1])
    me, core = lax.axis_index("pb"), lax.rem(lax.axis_index("ao"), 2)
    place = jnp.stack([me, core])

    def send(block, *targets):
        route = []
        for i in range(blocks):
            for m in range(members):
                target = targets[m % 2](i)
                if target is not None and 0 <= target[0] < blocks:
                    route.append((i * members + m, target[0] * members + m // 2 * 2 + target[1]))
        return lax.ppermute(block, ("pb", "ao"), route)

    sign = lambda i: 1 - 2 * (i % 2)
    partner = lambda c: lambda i: (i + sign(i), c)
    front = lambda c: lambda i: (i + 2 * sign(i), c)
    back = lambda c: lambda i: (i - 2 * sign(i), c)
    nobody = lambda i: None

    near = send(coefs, partner(0), back(1))
    query_t = send(queries, back(0), partner(1))
    far_1 = send(coefs, nobody, front(1))
    centre_own = lax.all_gather(centres, "ao", axis=0, tiled=True)
    centre_near = send(after(centre_own, query_t), back(1), partner(0))

    at_me, at_target, at_near, at_far = (0, 0), (2, 1), (1, 2), (2, -2)
    pairs = ((at_target, at_me), (at_target, at_near), (at_me, at_me), (at_me, at_near), (at_me, at_far))
    cut_rows = cut_values(place, pattern, pairs, radius)

    def kern(order, queries, query_at, centres, at, *scored):
        cuts = tuple(pairs.index((query_at, centre_at)) for centre_at in at)
        return kern_blocks(after(cut_rows, *order), queries, centres, cuts, *scored)

    width = coefs.shape[1] // 2
    coefs_hbm = pltpu.with_memory_space_constraint(coefs, pltpu.HBM)
    base_t = kern((), query_t, at_target, [[centre_own]], [at_me], [coefs_hbm])
    centre_far_1 = send(after(centre_own, base_t), nobody, front(1))
    kern_t = kern((base_t,), query_t, at_target, [[centre_near]], [at_near])
    far_0 = send(after(coefs, kern_t), back(0), nobody)
    near = after(near, kern_t)
    total, part = [], []
    for h in range(2):
        if h == 1:
            near = after(near, total[0], far_1, centre_far_1)
        total.append(scores([kern_t], [near], ((0, 0, 0, h * width, width),), BF16, base_t, h * width))
        part.append(send(total[h], front(0), partner(1)))
    centre_far_0 = send(after(centre_near, total[1]), nobody, lambda i: (i, 0))
    own, far_1 = kern(
        (total[1],), queries, at_me, [[centre_own], [centre_near]], [at_me, at_near], [coefs_hbm, near], F32, [far_1]
    )
    kern_far = kern((own,), queries, at_me, [[centre_far_0, centre_far_1]], [at_far])
    scale = 4.0 / radius**5
    out, rest = far_sum(place, kern_far, far_0, far_1, own, part[0], scale)
    return final(rest, part[1], scale, out)


def solution(mesh):
    in_specs = (P("pb", None), P(("pb", "ao"), None), P("pb", "ao"), P())
    out_specs = P("pb", "ao")
    return jax.shard_map(
        per_device, mesh=mesh, in_specs=in_specs, out_specs=out_specs, check_vma=False
    )
```

```python
import functools
import math

import jax
import jax.numpy as jnp
from jax import lax
from jax.experimental import pallas as pl
from jax.experimental.pallas import tpu as pltpu
from jax.sharding import PartitionSpec as P

RADIUS_FACTOR = 1.3
VMEM_LIMIT = 24 * 1024 * 1024
BF16 = jnp.bfloat16
F32 = jnp.float32
SMEM = pl.BlockSpec(memory_space=pltpu.SMEM)
WHOLE = pl.BlockSpec(memory_space=pltpu.VMEM)
ANY = pl.BlockSpec(memory_space=pl.ANY)


COST = pl.CostEstimate(flops=1 << 20, bytes_accessed=1 << 16, transcendentals=0)


def three_terms(norm):
    high = norm.astype(BF16).astype(F32)
    middle = (norm - high).astype(BF16).astype(F32)
    return high, middle, norm - high - middle


def widened(rows, centre_side):
    wide = rows.astype(F32)
    high, middle, low = three_terms(jnp.sum(wide * wide, axis=1, keepdims=True))
    lane = lax.broadcasted_iota(jnp.int32, (rows.shape[0], 128), 1)
    first, ones = (3, 0) if centre_side else (0, 3)
    extra = jnp.where((lane >= ones) & (lane < ones + 3), 1.0, 0.0)
    extra = jnp.where(lane == first, high, extra)
    extra = jnp.where(lane == first + 1, middle, extra)
    extra = jnp.where(lane == first + 2, low, extra)
    own = (wide * -2.0).astype(BF16) if centre_side else rows
    return jnp.concatenate([own, extra.astype(BF16)], axis=1)


def in_vmem(*arrays):
    return [pltpu.with_memory_space_constraint(array, pltpu.VMEM) for array in arrays]


def cut_kernel(radius, pairs, place_ref, pattern_ref, out_ref):
    me, core = place_ref[0], place_ref[1]
    side = 1 - 2 * lax.rem(me, 2)
    blocks, band = pattern_ref.shape
    for k, pair in enumerate(pairs):
        query_block, centre_block = (me + side * jnp.where(core == 0, step[0], step[1]) for step in pair)
        query_block = jnp.clip(query_block, 0, blocks - 1)
        offset = jnp.clip(centre_block - query_block + band // 2, 0, band - 1)
        cut = jnp.where(pattern_ref[query_block, offset] > 0, jnp.float32(radius), jnp.float32(-1.0))
        out_ref[k] = jnp.full(out_ref.shape[1:], cut, F32)


def cut_values(place, pattern, pairs, radius):
    return pl.pallas_call(
        functools.partial(cut_kernel, radius, pairs),
        in_specs=[SMEM, SMEM],
        out_specs=WHOLE,
        out_shape=pltpu.VMEM((len(pairs), 8, 512), F32),
        compiler_params=pltpu.CompilerParams(vmem_limit_bytes=VMEM_LIMIT),
        cost_estimate=COST,
        name="cuts",
    )(place, pattern)


def kern_tile(query, centre_wide, cut_ref, radius, out_ref, column):
    depth = centre_wide.shape[0]
    columns = min(512, depth)
    for start in range(0, depth, columns):
        square = lax.dot_general(
            query, centre_wide[pl.ds(start, columns), :], (((1,), (1,)), ((), ())), preferred_element_type=F32
        )
        square = jnp.maximum(square, 1e-30)
        dist = square * lax.rsqrt(square)
        inner = jnp.maximum(cut_ref[:1, :columns] - dist, 0.0)
        inner = inner * inner
        out_ref[:, pl.ds(column + start, columns)] = (inner * inner * (dist + radius / 4)).astype(BF16)


def kern_kernel(radius, cuts, sources, scored, carried, cut_ref, query_ref, *refs):
    blocks = len(cuts)
    centres, refs = refs[: blocks * sources], refs[blocks * sources :]
    coefs, refs = refs[: blocks * scored], refs[blocks * scored :]
    carry, refs = refs[:carried], refs[carried:]
    out_ref, *carry_out = refs[: 1 + carried]
    query_wide, centre_wide, *scratch = refs[1 + carried :]
    copies = []
    if scored:
        kern_ref, coef_ref, sems = scratch
        depth = centre_wide.shape[1]
        for b, coef in enumerate(coefs):
            copies.append(pltpu.make_async_copy(coef, coef_ref.at[pl.ds(b * depth, depth), :], sems.at[b]))
        for source, target in zip(carry, carry_out):
            copies.append(pltpu.make_async_copy(source, target, sems.at[blocks]))
    for copy in copies:
        copy.start()

    query_wide[...] = widened(query_ref[...], False)
    for b in range(blocks):
        centre = centres[b * sources][...]
        for source in centres[b * sources + 1 : (b + 1) * sources]:
            centre = centre + source[...]
        centre_wide[b] = widened(centre, True)

    tile = min(512, query_wide.shape[0])
    for row in range(query_wide.shape[0] // tile):
        rows = pl.ds(row * tile, tile)
        values = kern_ref if scored else out_ref.at[rows, :]
        for b, cut in enumerate(cuts):
            kern_tile(query_wide[rows, :], centre_wide.at[b], cut_ref.at[cut], radius, values, b * centre_wide.shape[1])
        if row == 0:
            for copy in copies:
                copy.wait()
        if scored:
            total = jnp.dot(kern_ref[...], coef_ref[...], preferred_element_type=F32)
            out_ref[rows, :] = total.astype(out_ref.dtype)


def kern_blocks(cut_rows, queries, centres, cuts, coefs=(), dtype=BF16, carry=()):
    query_rows, features = queries.shape
    blocks, centre_rows = len(centres), centres[0][0].shape[0]
    scratch = [
        pltpu.VMEM((query_rows, features + 128), BF16),
        pltpu.VMEM((blocks, centre_rows, features + 128), BF16),
    ]
    out_shape = [pltpu.VMEM((query_rows, blocks * centre_rows), BF16)]
    if coefs:
        width = coefs[0].shape[1]
        out_shape = [pltpu.VMEM((query_rows, width), dtype)]
        scratch += [
            pltpu.VMEM((min(512, query_rows), blocks * centre_rows), BF16),
            pltpu.VMEM((blocks * centre_rows, width), BF16),
            pltpu.SemaphoreType.DMA((blocks + 1,)),
        ]
    out_shape += [pltpu.VMEM(array.shape, array.dtype) for array in carry]
    pieces = [source for block in centres for source in block]
    out = pl.pallas_call(
        functools.partial(
            kern_kernel, RADIUS_FACTOR * math.sqrt(features), cuts, len(centres[0]), len(coefs) > 0, len(carry)
        ),
        in_specs=[WHOLE] * (2 + len(pieces)) + [ANY] * (len(coefs) + len(carry)),
        out_specs=[WHOLE] * len(out_shape),
        out_shape=out_shape,
        scratch_shapes=scratch,
        compiler_params=pltpu.CompilerParams(vmem_limit_bytes=VMEM_LIMIT),
        cost_estimate=COST,
        name="kern",
    )(cut_rows, queries, *pieces, *coefs, *carry)
    return out if carry else out[0]


def score_sum(terms, kern_refs, coef_refs, rows):
    total = None
    for kern, block, coef, column, width in terms:
        depth = coef_refs[coef].shape[0]
        product = jnp.dot(
            kern_refs[kern][rows, pl.ds(block * depth, depth)],
            coef_refs[coef][:, pl.ds(column, width)],
            preferred_element_type=F32,
        )
        total = product if total is None else total + product
    return total


def score_kernel(terms, kerns, adds, column, tile, *refs):
    out_ref = refs[-1]
    coefs = refs[kerns : len(refs) - 1 - adds]

    for row in range(out_ref.shape[0] // tile):
        rows = pl.ds(row * tile, tile)
        total = score_sum(terms, refs[:kerns], coefs, rows)
        if adds:
            total = total + refs[-2][rows, pl.ds(column, total.shape[1])].astype(F32)
        out_ref[rows, :] = total.astype(out_ref.dtype)


def scores(kerns, coefs, terms, dtype, add=None, column=0):
    rows, width = kerns[0].shape[0], terms[0][4]
    adds = [] if add is None else [add]
    return pl.pallas_call(
        functools.partial(score_kernel, terms, len(kerns), len(adds), column, min(512, rows)),
        in_specs=[WHOLE] * (len(kerns) + len(coefs) + len(adds)),
        out_specs=WHOLE,
        out_shape=pltpu.VMEM((rows, width), dtype),
        compiler_params=pltpu.CompilerParams(vmem_limit_bytes=VMEM_LIMIT),
        cost_estimate=COST,
        name="scores",
    )(*in_vmem(*kerns, *coefs, *adds))


def far_kernel(
    scale, place_ref, kern_ref, far_0_ref, far_1_ref, add_ref, part_ref, out_ref, rest_ref, low_ref, sems
):
    width = part_ref.shape[1]
    tile = min(512, kern_ref.shape[0])
    tiles = [pl.ds(row * tile, tile) for row in range(kern_ref.shape[0] // tile)]
    low, high = pl.ds(0, width), pl.ds(width, add_ref.shape[1] - width)

    def sums(coef_ref):
        copies = []
        for k, rows in enumerate(tiles):
            total = jnp.dot(kern_ref[rows, :], coef_ref[:, low], preferred_element_type=F32)
            total = total + add_ref[rows, low] + part_ref[rows, :].astype(F32)
            low_ref[rows, :] = (total * scale).astype(low_ref.dtype)
            copies.append(pltpu.make_async_copy(low_ref.at[rows, :], out_ref.at[rows, low], sems.at[k]))
            copies[k].start()
        for rows in tiles:
            total = jnp.dot(kern_ref[rows, :], coef_ref[:, high], preferred_element_type=F32)
            rest_ref[rows, :] = total + add_ref[rows, high]
        for copy in copies:
            copy.wait()

    @pl.when(place_ref[1] == 0)
    def _():
        sums(far_0_ref)

    @pl.when(place_ref[1] == 1)
    def _():
        sums(far_1_ref)


def far_sum(place, kern, far_0, far_1, add, part, scale):
    rows, width = part.shape
    return pl.pallas_call(
        functools.partial(far_kernel, scale),
        in_specs=[SMEM] + [WHOLE] * 5,
        out_specs=[ANY, WHOLE],
        out_shape=[jax.ShapeDtypeStruct(add.shape, BF16), pltpu.VMEM((rows, add.shape[1] - width), F32)],
        scratch_shapes=[
            pltpu.VMEM((rows, width), BF16),
            pltpu.SemaphoreType.DMA((rows // min(512, rows),)),
        ],
        compiler_params=pltpu.CompilerParams(vmem_limit_bytes=VMEM_LIMIT),
        cost_estimate=COST,
        name="far",
    )(place, *in_vmem(kern, far_0, far_1, add, part))


def final_kernel(scale, add_ref, part_ref, _, out_ref, last_ref, sems):
    rows, width = part_ref.shape
    tile = min(256, rows)
    columns = pl.ds(out_ref.shape[1] - width, width)
    copies = []
    for k in range(rows // tile):
        span = pl.ds(k * tile, tile)
        total = part_ref[span, :].astype(F32) + add_ref[span, :]
        last_ref[span, :] = (total * scale).astype(last_ref.dtype)
        copies.append(pltpu.make_async_copy(last_ref.at[span, :], out_ref.at[span, columns], sems.at[k]))
        copies[k].start()
    for copy in copies:
        copy.wait()


def final(add, part, scale, out):
    rows, width = part.shape
    return pl.pallas_call(
        functools.partial(final_kernel, scale),
        in_specs=[WHOLE, WHOLE, ANY],
        out_specs=ANY,
        out_shape=jax.ShapeDtypeStruct(out.shape, out.dtype),
        input_output_aliases={2: 0},
        scratch_shapes=[
            pltpu.VMEM((rows, width), BF16),
            pltpu.SemaphoreType.DMA((rows // min(256, rows),)),
        ],
        compiler_params=pltpu.CompilerParams(vmem_limit_bytes=VMEM_LIMIT),
        cost_estimate=COST,
        name="final",
    )(*in_vmem(add, part), out)


def after(array, *others):
    return lax.optimization_barrier((array, *others))[0]


def per_device(queries, centres, coefs, pattern):
    blocks, members = lax.axis_size("pb"), lax.axis_size("ao")
    radius = RADIUS_FACTOR * math.sqrt(queries.shape[1])
    me, core = lax.axis_index("pb"), lax.rem(lax.axis_index("ao"), 2)
    place = jnp.stack([me, core])

    def send(block, *targets):
        route = []
        for i in range(blocks):
            for m in range(members):
                target = targets[m % 2](i)
                if target is not None and 0 <= target[0] < blocks:
                    route.append((i * members + m, target[0] * members + m // 2 * 2 + target[1]))
        return lax.ppermute(block, ("pb", "ao"), route)

    sign = lambda i: 1 - 2 * (i % 2)
    partner = lambda c: lambda i: (i + sign(i), c)
    front = lambda c: lambda i: (i + 2 * sign(i), c)
    back = lambda c: lambda i: (i - 2 * sign(i), c)
    nobody = lambda i: None

    near = send(coefs, partner(0), back(1))
    query_t = send(queries, back(0), partner(1))
    far_1 = send(coefs, nobody, front(1))
    centre_own = lax.all_gather(centres, "ao", axis=0, tiled=True)
    centre_near = send(after(centre_own, query_t), back(1), partner(0))

    at_me, at_target, at_near, at_far = (0, 0), (2, 1), (1, 2), (2, -2)
    pairs = ((at_target, at_me), (at_target, at_near), (at_me, at_me), (at_me, at_near), (at_me, at_far))
    cut_rows = cut_values(place, pattern, pairs, radius)

    def kern(order, queries, query_at, centres, at, *scored):
        cuts = tuple(pairs.index((query_at, centre_at)) for centre_at in at)
        return kern_blocks(after(cut_rows, *order), queries, centres, cuts, *scored)

    whole = coefs.shape[1]
    first = whole * 5 // 8 if whole % 1024 == 0 else whole // 2
    coefs_hbm = pltpu.with_memory_space_constraint(coefs, pltpu.HBM)
    base_t = kern((), query_t, at_target, [[centre_own]], [at_me], [coefs_hbm])
    centre_far_1 = send(after(centre_own, base_t), nobody, front(1))
    kern_t = kern((base_t,), query_t, at_target, [[centre_near]], [at_near])
    far_0 = send(after(coefs, kern_t), back(0), nobody)
    near = after(near, kern_t)
    total, part = [], []
    for h, (column, width) in enumerate(((0, first), (first, whole - first))):
        if h == 1:
            near = after(near, total[0], far_1, centre_far_1)
        total.append(scores([kern_t], [near], ((0, 0, 0, column, width),), BF16, base_t, column))
        part.append(send(total[h], front(0), partner(1)))
    centre_far_0 = send(after(centre_near, total[1]), nobody, lambda i: (i, 0))
    own, far_1 = kern(
        (total[1],), queries, at_me, [[centre_own], [centre_near]], [at_me, at_near], [coefs_hbm, near], F32, [far_1]
    )
    kern_far = kern((own,), queries, at_me, [[centre_far_0, centre_far_1]], [at_far])
    scale = 4.0 / radius**5
    out, rest = far_sum(place, kern_far, far_0, far_1, own, part[0], scale)
    return final(rest, part[1], scale, out)


def solution(mesh):
    in_specs = (P("pb", None), P(("pb", "ao"), None), P("pb", "ao"), P())
    out_specs = P("pb", "ao")
    return jax.shard_map(
        per_device, mesh=mesh, in_specs=in_specs, out_specs=out_specs, check_vma=False
    )
```
